32 devices in a mesh: cand: 16 (over z, y, core), head: 2 (over x).
Axes of the slice: x: 2, y: 2, z: 4, core: 2. Of those that a mesh axis runs over, the one named last changes fastest.
Arguments:
- item_feats: bfloat16 [16384, 1024], P('cand', 'head'), may hold values from -6 to 6
- event_feats: bfloat16 [32, 64, 1024], P('cand', None, 'head'), may hold values from -6 to 6
- memory_cache: bfloat16 [32, 8, 128, 128], P('cand', 'head'), may hold values from -36 to 36
- norm_cache: bfloat16 [32, 8, 128], P('cand', 'head'), may hold values from -6 to 6
- query_weight: bfloat16 [1024, 1024], P(None, 'head'), may hold values from -0.1875 to 0.1875
- key_weight: bfloat16 [1024, 1024], P(None, 'head'), may hold values from -0.1875 to 0.1875
- value_weight: bfloat16 [1024, 1024], P(None, 'head'), may hold values from -0.1875 to 0.1875
- gate_weight: bfloat16 [2, 1024, 8], P(None, None, 'head'), may hold values from -0.1875 to 0.1875
- input_bias: float32 [8], P('head'), may hold values from -2 to 2
- forget_bias: float32 [8], P('head'), may hold values from 1 to 7
- head_gain: float32 [8, 128], P('head'), may hold values from 0.4 to 1.6
- tile_list: int32 [32, 4, 2], P('cand'), may hold values from 0 to 127, as said below
Outputs:
- new_memory: bfloat16 [32, 8, 128, 128], P('cand', 'head')
- new_norm: bfloat16 [32, 8, 128], P('cand', 'head')
- scores: float32 [32, 1024], P('cand', 'head')
The draws below stay inside these ranges and needn't reach their ends.
Inputs may be any that keep to these rules, and one draw needn't show every extreme that they name: `tile_list`: the 2 tiles of a group differ and lie in one block of 8 tiles (the tiles of one index of cand); the groups of a user lie in different blocks. The groups of the users of one index of cand name one block at most 2 times, and some block exactly 2 times. All users' groups name one block at most 16 times, and some block exactly 16 times.
All inputs are finite; a program needn't handle non-finite values.
Results may differ from the reference program's by a relative error of at most 0.0059.
Values may be sent and summed in bfloat16 or wider, within the bound.
A program may use at most 64 MiB of HBM per device.

```python
import math
import jax
import jax.numpy as jnp
from jax import lax

D = 1024
H = 8
DH = 128
TILE = 128
TILES_DEV = 8
TPD = 2
GROUPS = 4
CAP = 2
EVENTS = 64
USERS = 32
POOL_TILES = 128
POOL = 16384
CANDS_USER = 1024


def draw_memory_cache(key, part):
    key = jax.random.fold_in(key, 11)
    key_base, key_rows, key_cols = jax.random.split(key, 3)
    base = jnp.clip(jax.random.normal(key_base, (USERS, H, DH, DH), jnp.float32), -4.0, 4.0)
    row_scale = jnp.exp(jax.random.uniform(key_rows, (USERS, H, DH, 1), jnp.float32, -1.2, 1.09))
    col_scale = jnp.exp(jax.random.uniform(key_cols, (USERS, H, 1, DH), jnp.float32, -1.2, 1.09))
    return (base * row_scale * col_scale).astype(jnp.bfloat16)


def draw_tile_list(key, part):
    key = jax.random.fold_in(key, 23)
    ncand = POOL_TILES // TILES_DEV
    users_dev = USERS // ncand
    pairs = users_dev * GROUPS
    hot = ncand // 8
    span = ncand - hot
    live = (pairs - hot) // CAP
    key_rho, key_order, key_users, key_tiles = jax.random.split(key, 4)
    rho = jax.random.permutation(key_rho, ncand).astype(jnp.int32)
    source = jnp.arange(ncand, dtype=jnp.int32)
    ranks = jnp.arange(ncand, dtype=jnp.int32)
    cold_pos = (ranks[None, :] - hot - source[:, None]) % span
    counts = jnp.where(ranks[None, :] < hot, 1, jnp.where(cold_pos < live, CAP, 0)).astype(jnp.int32)
    order = jax.vmap(lambda k: jax.random.permutation(k, ncand))(jax.random.split(key_order, ncand)).astype(jnp.int32)
    counts_ord = jnp.take_along_axis(counts, order, axis=1)
    cum = jnp.cumsum(counts_ord, axis=1)
    element = jnp.arange(pairs, dtype=jnp.int32)
    position = jnp.sum((cum[:, None, :] <= element[None, :, None]).astype(jnp.int32), axis=-1).astype(jnp.int32)
    rank_of = jnp.take_along_axis(order, position, axis=1)
    dest = rho[rank_of]
    user_perm = jax.vmap(lambda k: jax.random.permutation(k, users_dev))(jax.random.split(key_users, ncand)).astype(jnp.int32)
    user_of = user_perm[:, element % users_dev]
    group_of = jnp.broadcast_to(element // users_dev, (ncand, pairs))
    source_of = jnp.broadcast_to(source[:, None], (ncand, pairs))
    table = jnp.zeros((ncand, users_dev, GROUPS), jnp.int32).at[source_of, user_of, group_of].set(dest)
    local = jax.vmap(lambda k: jax.random.permutation(k, TILES_DEV)[:TPD])(jax.random.split(key_tiles, ncand * users_dev * GROUPS)).astype(jnp.int32)
    local = local.reshape(ncand, users_dev, GROUPS, TPD)
    tiles = table[..., None] * TILES_DEV + local
    return tiles.reshape(USERS, GROUPS, TPD).astype(jnp.int32)


def steps_of(own_key, dims, cuts, smallest, top_value):
    gain = 1.0
    for dim, blocks in cuts:
        steps = jax.random.uniform(jax.random.fold_in(jax.random.fold_in(own_key, 6), dim), (blocks,), jnp.float32, smallest / len(cuts), top_value / len(cuts))
        gain = gain * jnp.repeat(jnp.exp(steps), dims[dim] // blocks).reshape((-1,) + (1,) * (len(dims) - 1 - dim))
    return gain


def noise(rng, extent, deviation, reach, cuts=(), kind=jnp.bfloat16):
    entries = deviation * jax.random.normal(rng, extent, jnp.float32)
    if cuts:
        entries = entries * steps_of(rng, extent, cuts, -0.22, 0.18)
    return jnp.clip(entries, -reach, reach).astype(kind)


def setup_inputs(seed: int = 0) -> dict:
    key_list = jax.random.split(jax.random.key(seed), 13)
    return {
        "item_feats": noise(key_list[0], (POOL, D), 1.0, 6.0, ((0, 16), (1, 2))),
        "event_feats": noise(key_list[1], (USERS, EVENTS, D), 1.0, 6.0, ((0, 16), (2, 2))),
        "memory_cache": draw_memory_cache(jax.random.fold_in(key_list[12], 71), 0),
        "norm_cache": noise(key_list[3], (USERS, H, DH), 1.0, 6.0, ((0, 16), (1, 2))),
        "query_weight": noise(key_list[4], (D, D), D ** -0.5, 0.1875, ((1, 2),)),
        "key_weight": noise(key_list[5], (D, D), D ** -0.5, 0.1875, ((1, 2),)),
        "value_weight": noise(key_list[6], (D, D), D ** -0.5, 0.1875, ((1, 2),)),
        "gate_weight": noise(key_list[7], (2, D, H), D ** -0.5, 0.1875, ((2, 2),)),
        "input_bias": jnp.clip(jax.random.uniform(key_list[8], (H,), jnp.float32, -2.0, 2.0) * steps_of(key_list[8], (H,), ((0, 2),), -0.4, 0.0), -2.0, 2.0),
        "forget_bias": jnp.clip(1.0 + 6.0 * jax.random.uniform(key_list[9], (H,), jnp.float32) ** steps_of(key_list[9], (H,), ((0, 2),), -0.2, 0.2), 1.0, 7.0),
        "head_gain": jnp.clip(1.0 + 0.12 * jax.random.normal(key_list[10], (H, DH), jnp.float32), 0.4, 1.6),
        "tile_list": draw_tile_list(jax.random.fold_in(key_list[12], 71), 0),
    }


def score_user(queries, item_feats, head_gain, memory, normalizer, tiles):
    items = (tiles[:, :, None] * TILE + jnp.arange(TILE, dtype=jnp.int32)[None, None, :]).reshape(-1).astype(jnp.int32)
    picked = queries[items].astype(jnp.float32)
    feats = item_feats[items].reshape(CANDS_USER, H, DH).astype(jnp.float32)
    numer = jnp.einsum('chj,hij->chi', picked, memory.astype(jnp.float32), precision=lax.Precision.HIGHEST)
    denom = jnp.einsum('chj,hj->ch', picked, normalizer.astype(jnp.float32), precision=lax.Precision.HIGHEST)
    normed = numer * lax.rsqrt(lax.optimization_barrier(jnp.mean(numer * numer, axis=-1, keepdims=True)) + 1e-05) * head_gain
    normed = normed / jnp.maximum(jnp.abs(denom), 1.0)[..., None]
    return lax.optimization_barrier(jnp.sum(normed * feats, axis=(1, 2))) / math.sqrt(D)

def reference(item_feats, event_feats, memory_cache, norm_cache, query_weight, key_weight, value_weight, gate_weight, input_bias, forget_bias, head_gain, tile_list):
    rows = event_feats.reshape(USERS * EVENTS, D)
    keys = (jnp.dot(rows, key_weight, preferred_element_type=jnp.float32) / math.sqrt(DH)).reshape(USERS, EVENTS, H, DH)
    values = jnp.dot(rows, value_weight, preferred_element_type=jnp.float32).reshape(USERS, EVENTS, H, DH)
    pre_input = jnp.dot(rows, gate_weight[0], preferred_element_type=jnp.float32).reshape(USERS, EVENTS, H) + input_bias
    pre_forget = jnp.dot(rows, gate_weight[1], preferred_element_type=jnp.float32).reshape(USERS, EVENTS, H) + forget_bias
    input_gate = jax.nn.sigmoid(pre_input)
    cum = jnp.cumsum(jax.nn.log_sigmoid(pre_forget), axis=1)
    weight = input_gate * jnp.exp(cum[:, -1:, :] - cum)
    carry = jnp.exp(cum[:, -1, :])
    update = jnp.einsum('uthi,uthj->uhij', weight[..., None] * values, keys, precision=lax.Precision.HIGHEST)
    new_memory = (carry[:, :, None, None] * memory_cache.astype(jnp.float32) + update).astype(jnp.bfloat16)
    norm_add = jnp.einsum('uth,uthj->uhj', weight, keys, precision=lax.Precision.HIGHEST)
    new_norm = (carry[:, :, None] * norm_cache.astype(jnp.float32) + norm_add).astype(jnp.bfloat16)
    queries = (jnp.dot(item_feats, query_weight, preferred_element_type=jnp.float32) / math.sqrt(DH)).astype(jnp.bfloat16)
    queries = queries.reshape(POOL, H, DH)

    def one_user(packed):
        return score_user(queries, item_feats, head_gain, packed[0], packed[1], packed[2])
    scores = lax.map(one_user, (new_memory, new_norm, tile_list))
    return (new_memory, new_norm, scores)
```

```python
import functools
import math

import jax
import jax.numpy as jnp
from jax import lax
from jax.experimental import pallas as pl
from jax.experimental.pallas import tpu as pltpu
from jax.sharding import PartitionSpec as P

DH = 128
TILE = 128
TILES_DEV = 8
TPD = 2
GROUPS = 4
PAD = 16
HI = lax.Precision.HIGHEST
MESH = pl.DeviceIdType.MESH


def dot(a, b, precision=None):
    return jnp.dot(a, b, preferred_element_type=jnp.float32, precision=precision)


def kernel(
    n_cand, n_head, users, events, heads, full_width,
    ev_ref, item_ref, mem_ref, nrm_ref, wq_ref, wk_ref, wv_ref, gate_ref, bias_ref, gain_ref, tl_ref, own_tl,
    nm_ref, nn_ref, sc_ref,
    ev, feats, wq, wk, wv, blocks, queries, weighted, tl_all, tl_s, scores, got,
    in_sem, ev_send, ev_recv, item_send, item_recv, tl_send, tl_recv, tl_sem,
    send_sem, recv_sem, back_send, back_recv,
):
    me = lax.axis_index("cand")
    head = lax.axis_index("head")
    core = me % 2
    col = (me // 2) % 2
    line = me // 4
    n_line = n_cand // 4
    width = heads * DH
    rows = users * events
    n_tiles = feats.shape[1] // TILE
    part = full_width // n_head
    norm_row = users * heads * DH

    def source(z, y, k):
        return z * 4 + y * 2 + k

    loads = [
        pltpu.make_async_copy(ev_ref, ev.at[head], in_sem.at[0]),
        pltpu.make_async_copy(wk_ref, wk, in_sem.at[1]),
        pltpu.make_async_copy(wv_ref, wv, in_sem.at[2]),
        pltpu.make_async_copy(item_ref, feats.at[head], in_sem.at[3]),
        pltpu.make_async_copy(wq_ref, wq, in_sem.at[4]),
    ]
    for load in loads:
        load.start()

    barrier = pltpu.get_barrier_semaphore()

    def greet(d, carry):
        c, h = d // n_head, d % n_head

        @pl.when(jnp.logical_or(c != me, h != head))
        def _():
            pl.semaphore_signal(barrier, inc=1, device_id=(c, h), device_id_type=MESH)

        return carry

    lax.fori_loop(0, n_cand * n_head, greet, 0)
    pl.semaphore_wait(barrier, n_cand * n_head - 1)

    def ev_copy(off):
        return pltpu.make_async_remote_copy(
            src_ref=ev_ref, dst_ref=ev.at[head], send_sem=ev_send.at[off], recv_sem=ev_recv.at[head],
            device_id=(me, (head + off) % n_head), device_id_type=MESH,
        )

    for off in range(1, n_head):
        ev_copy(off).start()

    def tl_copy(c):
        return pltpu.make_async_remote_copy(
            src_ref=tl_ref, dst_ref=tl_all.at[me], send_sem=tl_send, recv_sem=tl_recv,
            device_id=(c, head), device_id_type=MESH,
        )

    def send_list(off, carry):
        tl_copy((me + off) % n_cand).start()
        return carry

    lax.fori_loop(1, n_cand, send_list, 0)
    pltpu.make_async_copy(tl_ref, tl_all.at[me], tl_recv).start()

    for off in range(1, n_head):
        src = (head + off) % n_head
        pltpu.make_async_copy(ev.at[src], ev.at[src], ev_recv.at[src]).wait()

    def item_copy(off, t):
        at = pl.ds(pl.multiple_of(t * TILE, TILE), TILE)
        return pltpu.make_async_remote_copy(
            src_ref=item_ref.at[at], dst_ref=feats.at[head, at],
            send_sem=item_send.at[off * n_tiles + t], recv_sem=item_recv.at[head * n_tiles + t],
            device_id=(me, (head + off) % n_head), device_id_type=MESH,
        )

    for t in range(n_tiles):
        for off in range(1, n_head):
            item_copy(off, t).start()

    for load in loads[:3]:
        load.wait()
    gates = jnp.zeros((2 * heads, rows), jnp.float32)
    keys = jnp.zeros((rows, width), jnp.float32)
    values = jnp.zeros((rows, width), jnp.float32)
    for hh in range(n_head):
        at = slice(hh * part, (hh + 1) * part)
        x = ev[hh]
        gates += lax.dot_general(
            gate_ref[:, at], x, (((1,), (1,)), ((), ())), preferred_element_type=jnp.float32
        )
        keys += dot(x, wk[at, :])
        values += dot(x, wv[at, :])
    gates += bias_ref[...]
    keys = keys * (1.0 / math.sqrt(DH))
    values_t = values.T
    forget = gates[heads:]
    log_forget = jnp.minimum(forget, 0.0) - jnp.log1p(jnp.exp(-jnp.abs(forget)))
    s_id = lax.broadcasted_iota(jnp.int32, (rows, rows), 0)
    t_id = lax.broadcasted_iota(jnp.int32, (rows, rows), 1)
    later = jnp.where((s_id > t_id) & (s_id // events == t_id // events), 1.0, 0.0)
    weight = jax.nn.sigmoid(gates[:heads]) * jnp.exp(dot(log_forget, later, HI))
    lane_user = lax.broadcasted_iota(jnp.int32, (heads, rows), 1) // events
    norms = []
    for u in range(users):
        mine = lane_user == u
        carry = jnp.exp(jnp.sum(jnp.where(mine, log_forget, 0.0), axis=1, keepdims=True))
        weight_u = jnp.where(mine, weight, 0.0)
        norm_add = dot(weight_u, keys, HI)
        norm_old = nrm_ref[u].astype(jnp.float32)
        for h in range(heads):
            at = slice(h * DH, (h + 1) * DH)
            update = dot(values_t[at, :] * weight_u[h : h + 1, :], keys[:, at], HI)
            new = carry[h : h + 1, :] * mem_ref[u, h].astype(jnp.float32) + update
            r = (u * heads + h) * DH
            blocks[me, r : r + DH, :] = new.astype(jnp.bfloat16)
            norms.append(carry[h : h + 1, :] * norm_old[h : h + 1, :] + norm_add[h : h + 1, at])
    norms.append(jnp.zeros((PAD - users * heads, DH), jnp.float32))
    blocks[me, norm_row : norm_row + PAD, :] = jnp.concatenate(norms, axis=0).astype(jnp.bfloat16)

    def send(src, way, c):
        return pltpu.make_async_remote_copy(
            src_ref=blocks.at[src], dst_ref=blocks.at[src],
            send_sem=send_sem.at[src * 4 + way], recv_sem=recv_sem.at[src],
            device_id=(c, head), device_id_type=MESH,
        )

    up = source(jnp.minimum(line + 1, n_line - 1), col, core)
    down = source(jnp.maximum(line - 1, 0), col, core)
    across = source(line, 1 - col, core)
    twin = source(line, col, 1 - core)

    def each_send(z, act):
        src = source(z, col, core)

        @pl.when((z <= line) & (line + 1 < n_line))
        def _():
            act(send(src, 0, up))

        @pl.when((z >= line) & (line >= 1))
        def _():
            act(send(src, 1, down))

        act(send(src, 2, across))
        act(send(src, 3, twin))

    def start(copy):
        copy.start()

    def arrived(src):
        pltpu.make_async_copy(blocks.at[src], blocks.at[src], recv_sem.at[src]).wait()

    near = jnp.minimum(line, n_line - 1 - line)
    far_sign = jnp.where(line < n_line - 1 - line, 1, -1)

    def order(n):
        paired = line + jnp.where(n % 2 == 1, -1, 1) * ((n + 1) // 2)
        return jnp.where(n <= 2 * near, paired, line + far_sign * (n - near))

    def from_across(n):
        src = source(order(n), 1 - col, core)
        arrived(src)
        send(src, 3, twin).start()

    each_send(line, start)

    for u in range(users):
        for h in range(heads):
            r = (u * heads + h) * DH
            nm_ref[u, h] = blocks[me, r : r + DH, :]
    final_norms = blocks[me, norm_row : norm_row + PAD, :].astype(jnp.float32)
    for u in range(users):
        nn_ref[u] = final_norms[u * heads : (u + 1) * heads, :].astype(jnp.bfloat16)

    loads[3].wait()
    loads[4].wait()

    def features(t, carry):
        at = pl.ds(pl.multiple_of(t * TILE, TILE), TILE)
        x = feats[head, at, :].astype(jnp.float32)
        for h in range(heads):
            c = slice(h * DH, (h + 1) * DH)
            weighted[t, c, :] = (x[:, c] * (gain_ref[h : h + 1, :] * (1.0 / math.sqrt(full_width)))).T
        return carry

    lax.fori_loop(0, n_tiles, features, 0)

    def project(t, carry):
        at = pl.ds(pl.multiple_of(t * TILE, TILE), TILE)
        for off in range(1, n_head):
            src = (head + off) % n_head
            pltpu.make_async_copy(
                feats.at[src, at], feats.at[src, at], item_recv.at[src * n_tiles + t]
            ).wait()
        acc = jnp.zeros((TILE, width), jnp.float32)
        for hh in range(n_head):
            acc += dot(feats[hh, at, :], wq[hh * part : (hh + 1) * part, :])
        acc = acc * (1.0 / math.sqrt(DH))
        for h in range(heads):
            c = slice(h * DH, (h + 1) * DH)
            queries[t, c, :] = acc[:, c].T.astype(jnp.bfloat16)
        return carry

    lax.fori_loop(0, n_tiles // n_line, project, 0)
    for s in range(1, n_line):

        @pl.when(line - s >= 0)
        def _():
            arrived(source(line - s, col, core))
            each_send(line - s, start)

        @pl.when(line + s < n_line)
        def _():
            arrived(source(line + s, col, core))
            each_send(line + s, start)

        from_across(jnp.int32(s - 1))
        lax.fori_loop(s * n_tiles // n_line, (s + 1) * n_tiles // n_line, project, 0)

    pltpu.make_async_copy(tl_all, tl_all, tl_recv).wait()
    to_smem = pltpu.make_async_copy(tl_all, tl_s, tl_sem)
    to_smem.start()
    to_smem.wait()

    def back_copy(src, h):
        return pltpu.make_async_remote_copy(
            src_ref=scores.at[src], dst_ref=got.at[head, me], send_sem=back_send, recv_sem=back_recv,
            device_id=(src, h), device_id_type=MESH,
        )

    def score(j, carry):
        @pl.when(j == 2 * n_line)
        def _():
            from_across(jnp.int32(n_line - 1))

        z = order(j % n_line)
        y = jnp.where(j < 2 * n_line, col, 1 - col)
        other = (j // n_line) % 2
        k = jnp.where(other == 0, core, 1 - core)
        src = source(z, y, k)

        @pl.when(other == 1)
        def _():
            arrived(src)

        norm_block = blocks[src, norm_row : norm_row + PAD, :]
        for u in range(users):
            picks = [jnp.int32(0), jnp.int32(0)]
            for g in range(GROUPS):
                first = tl_s[src, 0, (u * GROUPS + g) * TPD]
                hit = first // TILES_DEV == me
                for p in range(TPD):
                    tile = tl_s[src, 0, (u * GROUPS + g) * TPD + p]
                    picks[p] = jnp.where(hit, tile % TILES_DEV, picks[p])
            totals = [jnp.zeros((1, TILE), jnp.float32) for _ in range(TPD)]
            for h in range(heads):
                r = (u * heads + h) * DH
                left = jnp.concatenate([blocks[src, r : r + DH, :], norm_block], axis=0)
                c = slice(h * DH, (h + 1) * DH)
                for p in range(TPD):
                    product = dot(left, queries[picks[p], c, :])
                    numer = product[:DH]
                    i = DH + u * heads + h
                    denom = product[i : i + 1]
                    square = jnp.sum(numer * numer, axis=0, keepdims=True)
                    value = jnp.sum(numer * weighted[picks[p], c, :], axis=0, keepdims=True)
                    totals[p] += value * lax.rsqrt(square * (1.0 / DH) + 1e-05) / jnp.maximum(
                        jnp.abs(denom), 1.0
                    )
            for p in range(TPD):
                scores[src, u * TPD + p : u * TPD + p + 1, :] = totals[p]
        for h in range(n_head):
            here = (src == me) & (head == h)

            @pl.when(here)
            def _():
                pltpu.make_async_copy(scores.at[src], got.at[head, me], back_recv).start()

            @pl.when(jnp.logical_not(here))
            def _():
                back_copy(src, h).start()

        return carry

    lax.fori_loop(0, n_cand, score, 0)

    pltpu.make_async_copy(got, got, back_recv).wait()
    n_cols = GROUPS * TPD // n_head
    for u in range(users):
        for q in range(n_cols):
            m = head * n_cols + q
            first = own_tl[0, u * GROUPS * TPD + (m // TPD) * TPD]
            block = first // TILES_DEV
            total = jnp.zeros((TPD, TILE), jnp.float32)
            for hh in range(n_head):
                total += got[hh, block][u * TPD : (u + 1) * TPD]
            row = jnp.where(m % TPD == 0, total[0:1], total[1:2])
            sc_ref[u : u + 1, q * TILE : (q + 1) * TILE] = row

    for off in range(1, n_head):
        ev_copy(off).wait_send()

    def item_left(t, carry):
        for off in range(1, n_head):
            item_copy(off, t).wait_send()
        return carry

    lax.fori_loop(0, n_tiles, item_left, 0)
    rest = pl.ds(0, n_cand - 1)
    pltpu.make_async_copy(tl_all.at[rest], tl_all.at[rest], tl_send).wait()

    def left(copy):
        copy.wait_send()

    def blocks_left(z, carry):
        each_send(z, left)
        send(source(z, 1 - col, core), 3, twin).wait_send()
        return carry

    lax.fori_loop(0, n_line, blocks_left, 0)
    for h in range(n_head):
        here = head == h

        @pl.when(here)
        def _():
            pltpu.make_async_copy(scores.at[rest], scores.at[rest], back_send).wait()

        @pl.when(jnp.logical_not(here))
        def _():
            pltpu.make_async_copy(scores, scores, back_send).wait()


def on_device(
    item_feats, event_feats, memory_cache, norm_cache, query_weight, key_weight, value_weight,
    gate_weight, input_bias, forget_bias, head_gain, tile_list,
):
    n_cand = lax.axis_size("cand")
    n_head = lax.axis_size("head")
    users, events, part = event_feats.shape
    heads = memory_cache.shape[1]
    full_width, width = query_weight.shape
    pool = item_feats.shape[0]
    n_tiles = pool // TILE
    rows = users * events
    entries = users * GROUPS * TPD
    gates_t = jnp.transpose(gate_weight, (0, 2, 1)).reshape(2 * heads, full_width)
    bias = jnp.concatenate([input_bias, forget_bias])[:, None]
    tiles = jnp.pad(tile_list.reshape(1, entries), ((0, 0), (0, 128 - entries)))
    block_rows = users * heads * DH + PAD
    score_rows = max(8, users * TPD)
    vmem = pl.BlockSpec(memory_space=pltpu.VMEM)
    smem = pl.BlockSpec(memory_space=pltpu.SMEM)
    any_space = pl.BlockSpec(memory_space=pl.ANY)
    dma = pltpu.SemaphoreType.DMA
    new_memory, new_norm, scores = pl.pallas_call(
        functools.partial(kernel, n_cand, n_head, users, events, heads, full_width),
        out_shape=(
            jax.ShapeDtypeStruct(memory_cache.shape, jnp.bfloat16),
            jax.ShapeDtypeStruct(norm_cache.shape, jnp.bfloat16),
            jax.ShapeDtypeStruct((users, GROUPS * TPD * TILE // n_head), jnp.float32),
        ),
        in_specs=[any_space, any_space, vmem, vmem, any_space, any_space, any_space, vmem, vmem, vmem, vmem, smem],
        out_specs=(vmem, vmem, vmem),
        scratch_shapes=[
            pltpu.VMEM((n_head, rows, part), jnp.bfloat16),
            pltpu.VMEM((n_head, pool, part), jnp.bfloat16),
            pltpu.VMEM((full_width, width), jnp.bfloat16),
            pltpu.VMEM((full_width, width), jnp.bfloat16),
            pltpu.VMEM((full_width, width), jnp.bfloat16),
            pltpu.VMEM((n_cand, block_rows, DH), jnp.bfloat16),
            pltpu.VMEM((n_tiles, width, TILE), jnp.bfloat16),
            pltpu.VMEM((n_tiles, width, TILE), jnp.float32),
            pltpu.VMEM((n_cand, 1, 128), jnp.int32),
            pltpu.SMEM((n_cand, 1, 128), jnp.int32),
            pltpu.VMEM((n_cand, score_rows, TILE), jnp.float32),
            pltpu.VMEM((n_head, n_cand, score_rows, TILE), jnp.float32),
            dma((5,)),
            dma((n_head,)),
            dma((n_head,)),
            dma((n_head * n_tiles,)),
            dma((n_head * n_tiles,)),
            dma,
            dma,
            dma,
            dma((n_cand * 4,)),
            dma((n_cand,)),
            dma,
            dma,
        ],
        compiler_params=pltpu.CompilerParams(
            collective_id=0, has_side_effects=True, vmem_limit_bytes=48 * 1024 * 1024
        ),
    )(
        event_feats.reshape(rows, part), item_feats, memory_cache, norm_cache, query_weight, key_weight,
        value_weight, gates_t, bias, head_gain, tiles, tiles,
    )
    return new_memory, new_norm, scores


def solution(mesh):
    in_specs = (
        P("cand", "head"),
        P("cand", None, "head"),
        P("cand", "head", None, None),
        P("cand", "head", None),
        P(None, "head"),
        P(None, "head"),
        P(None, "head"),
        P(None, None, "head"),
        P("head"),
        P("head"),
        P("head", None),
        P("cand", None, None),
    )
    out_specs = (P("cand", "head", None, None), P("cand", "head", None), P("cand", "head"))
    return jax.shard_map(
        on_device, mesh=mesh, in_specs=in_specs, out_specs=out_specs, check_vma=False
    )
```

```python
import functools
import math

import jax
import jax.numpy as jnp
from jax import lax
from jax.experimental import pallas as pl
from jax.experimental.pallas import tpu as pltpu
from jax.sharding import PartitionSpec as P

DH = 128
TILE = 128
TILES_DEV = 8
TPD = 2
GROUPS = 4
PAD = 16
HI = lax.Precision.HIGHEST
MESH = pl.DeviceIdType.MESH


def dot(a, b, precision=None):
    return jnp.dot(a, b, preferred_element_type=jnp.float32, precision=precision)


def kernel(
    n_cand, n_head, users, events, heads, full_width,
    ev_ref, item_ref, mem_ref, nrm_ref, wq_ref, wk_ref, wv_ref, gate_ref, bias_i, bias_f, gain_ref, own_tl,
    nm_ref, nn_ref, sc_ref,
    ev, feats, wq, wk, wv, blocks, queries, weighted, tl_ref, tl_all, tl_s, scores, got,
    in_sem, ev_send, ev_recv, item_send, item_recv, tl_send, tl_recv, tl_sem,
    send_sem, recv_sem, back_send, back_recv,
):
    me = lax.axis_index("cand")
    head = lax.axis_index("head")
    core = me % 2
    col = (me // 2) % 2
    line = me // 4
    n_line = n_cand // 4
    width = heads * DH
    rows = users * events
    n_tiles = feats.shape[1] // TILE
    part = full_width // n_head
    norm_row = users * heads * DH

    def source(z, y, k):
        return z * 4 + y * 2 + k

    loads = [
        pltpu.make_async_copy(ev_ref, ev.at[head], in_sem.at[0]),
        pltpu.make_async_copy(wk_ref, wk, in_sem.at[1]),
        pltpu.make_async_copy(wv_ref, wv, in_sem.at[2]),
        pltpu.make_async_copy(item_ref, feats.at[head], in_sem.at[3]),
        pltpu.make_async_copy(wq_ref, wq, in_sem.at[4]),
    ]
    for load in loads:
        load.start()

    entry = lax.broadcasted_iota(jnp.int32, (1, 128), 1)
    own_row = jnp.zeros((1, 128), jnp.int32)
    for u in range(users):
        for g in range(GROUPS):
            for p in range(TPD):
                own_row = jnp.where(entry == (u * GROUPS + g) * TPD + p, own_tl[u, p, g], own_row)
    tl_ref[...] = own_row

    barrier = pltpu.get_barrier_semaphore()

    def greet(d, carry):
        c, h = d // n_head, d % n_head

        @pl.when(jnp.logical_or(c != me, h != head))
        def _():
            pl.semaphore_signal(barrier, inc=1, device_id=(c, h), device_id_type=MESH)

        return carry

    lax.fori_loop(0, n_cand * n_head, greet, 0)
    pl.semaphore_wait(barrier, n_cand * n_head - 1)

    def ev_copy(off):
        return pltpu.make_async_remote_copy(
            src_ref=ev_ref, dst_ref=ev.at[head], send_sem=ev_send.at[off], recv_sem=ev_recv.at[head],
            device_id=(me, (head + off) % n_head), device_id_type=MESH,
        )

    for off in range(1, n_head):
        ev_copy(off).start()

    def item_copy(off, t):
        at = pl.ds(pl.multiple_of(t * TILE, TILE), TILE)
        return pltpu.make_async_remote_copy(
            src_ref=item_ref.at[at], dst_ref=feats.at[head, at],
            send_sem=item_send.at[off * n_tiles + t], recv_sem=item_recv.at[head * n_tiles + t],
            device_id=(me, (head + off) % n_head), device_id_type=MESH,
        )

    for t in range(n_tiles):
        for off in range(1, n_head):
            item_copy(off, t).start()

    def tl_copy(c):
        return pltpu.make_async_remote_copy(
            src_ref=tl_ref, dst_ref=tl_all.at[me], send_sem=tl_send, recv_sem=tl_recv,
            device_id=(c, head), device_id_type=MESH,
        )

    def send_list(off, carry):
        tl_copy((me + off) % n_cand).start()
        return carry

    lax.fori_loop(1, n_cand, send_list, 0)
    pltpu.make_async_copy(tl_ref, tl_all.at[me], tl_recv).start()

    for off in range(1, n_head):
        src = (head + off) % n_head
        pltpu.make_async_copy(ev.at[src], ev.at[src], ev_recv.at[src]).wait()

    for load in loads[:3]:
        load.wait()
    pre = []
    for bias in (bias_i, bias_f):
        h_id = lax.broadcasted_iota(jnp.int32, (heads, rows), 0)
        column = jnp.zeros((heads, rows), jnp.float32)
        for h in range(heads):
            column = jnp.where(h_id == h, bias[h], column)
        pre.append(column)
    keys = jnp.zeros((rows, width), jnp.float32)
    values = jnp.zeros((rows, width), jnp.float32)
    for hh in range(n_head):
        at = slice(hh * part, (hh + 1) * part)
        x = ev[hh]
        for i in range(2):
            pre[i] += lax.dot_general(
                gate_ref[i, :, at], x, (((1,), (1,)), ((), ())), preferred_element_type=jnp.float32
            )
        keys += dot(x, wk[at, :])
        values += dot(x, wv[at, :])
    keys = keys * (1.0 / math.sqrt(DH))
    values_t = values.T
    forget = pre[1]
    log_forget = jnp.minimum(forget, 0.0) - jnp.log1p(jnp.exp(-jnp.abs(forget)))
    s_id = lax.broadcasted_iota(jnp.int32, (rows, rows), 0)
    t_id = lax.broadcasted_iota(jnp.int32, (rows, rows), 1)
    later = jnp.where((s_id > t_id) & (s_id // events == t_id // events), 1.0, 0.0)
    weight = jax.nn.sigmoid(pre[0]) * jnp.exp(dot(log_forget, later, HI))
    lane_user = lax.broadcasted_iota(jnp.int32, (heads, rows), 1) // events
    norms = []
    for u in range(users):
        mine = lane_user == u
        carry = jnp.exp(jnp.sum(jnp.where(mine, log_forget, 0.0), axis=1, keepdims=True))
        weight_u = jnp.where(mine, weight, 0.0)
        norm_add = dot(weight_u, keys, HI)
        norm_old = nrm_ref[u].astype(jnp.float32)
        for h in range(heads):
            at = slice(h * DH, (h + 1) * DH)
            update = dot(values_t[at, :] * weight_u[h : h + 1, :], keys[:, at], HI)
            new = carry[h : h + 1, :] * mem_ref[u, h].astype(jnp.float32) + update
            r = (u * heads + h) * DH
            blocks[me, r : r + DH, :] = new.astype(jnp.bfloat16)
            norms.append(carry[h : h + 1, :] * norm_old[h : h + 1, :] + norm_add[h : h + 1, at])
    norms.append(jnp.zeros((PAD - users * heads, DH), jnp.float32))
    blocks[me, norm_row : norm_row + PAD, :] = jnp.concatenate(norms, axis=0).astype(jnp.bfloat16)

    def send(src, way, c):
        return pltpu.make_async_remote_copy(
            src_ref=blocks.at[src], dst_ref=blocks.at[src],
            send_sem=send_sem.at[src * 4 + way], recv_sem=recv_sem.at[src],
            device_id=(c, head), device_id_type=MESH,
        )

    up = source(jnp.minimum(line + 1, n_line - 1), col, core)
    down = source(jnp.maximum(line - 1, 0), col, core)
    across = source(line, 1 - col, core)
    twin = source(line, col, 1 - core)

    def each_send(z, act):
        src = source(z, col, core)

        @pl.when((z <= line) & (line + 1 < n_line))
        def _():
            act(send(src, 0, up))

        @pl.when((z >= line) & (line >= 1))
        def _():
            act(send(src, 1, down))

        act(send(src, 2, across))
        act(send(src, 3, twin))

    def start(copy):
        copy.start()

    def arrived(src):
        pltpu.make_async_copy(blocks.at[src], blocks.at[src], recv_sem.at[src]).wait()

    near = jnp.minimum(line, n_line - 1 - line)
    far_sign = jnp.where(line < n_line - 1 - line, 1, -1)

    def order(n):
        paired = line + jnp.where(n % 2 == 1, -1, 1) * ((n + 1) // 2)
        return jnp.where(n <= 2 * near, paired, line + far_sign * (n - near))

    def from_across(n):
        src = source(order(n), 1 - col, core)
        arrived(src)
        send(src, 3, twin).start()

    each_send(line, start)

    for u in range(users):
        for h in range(heads):
            r = (u * heads + h) * DH
            nm_ref[u, h] = blocks[me, r : r + DH, :]
    final_norms = blocks[me, norm_row : norm_row + PAD, :].astype(jnp.float32)
    for u in range(users):
        nn_ref[u] = final_norms[u * heads : (u + 1) * heads, :].astype(jnp.bfloat16)

    loads[3].wait()
    loads[4].wait()

    def features(t, carry):
        at = pl.ds(pl.multiple_of(t * TILE, TILE), TILE)
        x = feats[head, at, :].astype(jnp.float32)
        for h in range(heads):
            c = slice(h * DH, (h + 1) * DH)
            weighted[t, c, :] = (x[:, c] * (gain_ref[h : h + 1, :] * (1.0 / math.sqrt(full_width)))).T
        return carry

    lax.fori_loop(0, n_tiles, features, 0)

    def project(t, carry):
        at = pl.ds(pl.multiple_of(t * TILE, TILE), TILE)
        for off in range(1, n_head):
            src = (head + off) % n_head
            pltpu.make_async_copy(
                feats.at[src, at], feats.at[src, at], item_recv.at[src * n_tiles + t]
            ).wait()
        acc = jnp.zeros((TILE, width), jnp.float32)
        for hh in range(n_head):
            acc += dot(feats[hh, at, :], wq[hh * part : (hh + 1) * part, :])
        acc = acc * (1.0 / math.sqrt(DH))
        for h in range(heads):
            c = slice(h * DH, (h + 1) * DH)
            queries[t, c, :] = acc[:, c].T.astype(jnp.bfloat16)
        return carry

    lax.fori_loop(0, n_tiles // n_line, project, 0)
    for s in range(1, n_line):

        @pl.when(line - s >= 0)
        def _():
            arrived(source(line - s, col, core))
            each_send(line - s, start)

        @pl.when(line + s < n_line)
        def _():
            arrived(source(line + s, col, core))
            each_send(line + s, start)

        from_across(jnp.int32(s - 1))
        lax.fori_loop(s * n_tiles // n_line, (s + 1) * n_tiles // n_line, project, 0)

    pltpu.make_async_copy(tl_all, tl_all, tl_recv).wait()
    to_smem = pltpu.make_async_copy(tl_all, tl_s, tl_sem)
    to_smem.start()
    to_smem.wait()

    def back_copy(src, h):
        return pltpu.make_async_remote_copy(
            src_ref=scores.at[src], dst_ref=got.at[head, me], send_sem=back_send, recv_sem=back_recv,
            device_id=(src, h), device_id_type=MESH,
        )

    def score(j, carry):
        @pl.when(j == 2 * n_line)
        def _():
            from_across(jnp.int32(n_line - 1))

        z = order(j % n_line)
        y = jnp.where(j < 2 * n_line, col, 1 - col)
        other = (j // n_line) % 2
        k = jnp.where(other == 0, core, 1 - core)
        src = source(z, y, k)

        @pl.when(other == 1)
        def _():
            arrived(src)

        norm_block = blocks[src, norm_row : norm_row + PAD, :]
        for u in range(users):
            picks = [jnp.int32(0), jnp.int32(0)]
            for g in range(GROUPS):
                first = tl_s[src, 0, (u * GROUPS + g) * TPD]
                hit = first // TILES_DEV == me
                for p in range(TPD):
                    tile = tl_s[src, 0, (u * GROUPS + g) * TPD + p]
                    picks[p] = jnp.where(hit, tile % TILES_DEV, picks[p])
            totals = [jnp.zeros((1, TILE), jnp.float32) for _ in range(TPD)]
            for h in range(heads):
                r = (u * heads + h) * DH
                left = jnp.concatenate([blocks[src, r : r + DH, :], norm_block], axis=0)
                c = slice(h * DH, (h + 1) * DH)
                for p in range(TPD):
                    product = dot(left, queries[picks[p], c, :])
                    numer = product[:DH]
                    i = DH + u * heads + h
                    denom = product[i : i + 1]
                    square = jnp.sum(numer * numer, axis=0, keepdims=True)
                    value = jnp.sum(numer * weighted[picks[p], c, :], axis=0, keepdims=True)
                    totals[p] += value * lax.rsqrt(square * (1.0 / DH) + 1e-05) / jnp.maximum(
                        jnp.abs(denom), 1.0
                    )
            for p in range(TPD):
                scores[src, u * TPD + p : u * TPD + p + 1, :] = totals[p]
        for h in range(n_head):
            here = (src == me) & (head == h)

            @pl.when(here)
            def _():
                pltpu.make_async_copy(scores.at[src], got.at[head, me], back_recv).start()

            @pl.when(jnp.logical_not(here))
            def _():
                back_copy(src, h).start()

        return carry

    lax.fori_loop(0, n_cand, score, 0)

    pltpu.make_async_copy(got, got, back_recv).wait()
    n_cols = GROUPS * TPD // n_head
    for u in range(users):
        for q in range(n_cols):
            m = head * n_cols + q
            first = own_tl[u, 0, m // TPD]
            block = first // TILES_DEV
            total = jnp.zeros((TPD, TILE), jnp.float32)
            for hh in range(n_head):
                total += got[hh, block][u * TPD : (u + 1) * TPD]
            row = jnp.where(m % TPD == 0, total[0:1], total[1:2])
            sc_ref[u : u + 1, q * TILE : (q + 1) * TILE] = row

    for off in range(1, n_head):
        ev_copy(off).wait_send()

    def item_left(t, carry):
        for off in range(1, n_head):
            item_copy(off, t).wait_send()
        return carry

    lax.fori_loop(0, n_tiles, item_left, 0)
    rest = pl.ds(0, n_cand - 1)
    pltpu.make_async_copy(tl_all.at[rest], tl_all.at[rest], tl_send).wait()

    def left(copy):
        copy.wait_send()

    def blocks_left(z, carry):
        each_send(z, left)
        send(source(z, 1 - col, core), 3, twin).wait_send()
        return carry

    lax.fori_loop(0, n_line, blocks_left, 0)
    for h in range(n_head):
        here = head == h

        @pl.when(here)
        def _():
            pltpu.make_async_copy(scores.at[rest], scores.at[rest], back_send).wait()

        @pl.when(jnp.logical_not(here))
        def _():
            pltpu.make_async_copy(scores, scores, back_send).wait()


def on_device(
    item_feats, event_feats, memory_cache, norm_cache, query_weight, key_weight, value_weight,
    gate_weight, input_bias, forget_bias, head_gain, tile_list,
):
    n_cand = lax.axis_size("cand")
    n_head = lax.axis_size("head")
    users, events, part = event_feats.shape
    heads = memory_cache.shape[1]
    full_width, width = query_weight.shape
    pool = item_feats.shape[0]
    n_tiles = pool // TILE
    rows = users * events
    gates_t = jnp.transpose(gate_weight, (0, 2, 1))
    tiles = jnp.transpose(tile_list, (0, 2, 1))
    block_rows = users * heads * DH + PAD
    score_rows = max(8, users * TPD)
    vmem = pl.BlockSpec(memory_space=pltpu.VMEM)
    smem = pl.BlockSpec(memory_space=pltpu.SMEM)
    any_space = pl.BlockSpec(memory_space=pltpu.HBM)
    dma = pltpu.SemaphoreType.DMA
    new_memory, new_norm, scores = pl.pallas_call(
        functools.partial(kernel, n_cand, n_head, users, events, heads, full_width),
        out_shape=(
            jax.ShapeDtypeStruct(memory_cache.shape, jnp.bfloat16),
            jax.ShapeDtypeStruct(norm_cache.shape, jnp.bfloat16),
            jax.ShapeDtypeStruct((users, GROUPS * TPD * TILE // n_head), jnp.float32),
        ),
        in_specs=[any_space, any_space, vmem, vmem, any_space, any_space, any_space, vmem, smem, smem, vmem, smem],
        out_specs=(vmem, vmem, vmem),
        scratch_shapes=[
            pltpu.VMEM((n_head, rows, part), jnp.bfloat16),
            pltpu.VMEM((n_head, pool, part), jnp.bfloat16),
            pltpu.VMEM((full_width, width), jnp.bfloat16),
            pltpu.VMEM((full_width, width), jnp.bfloat16),
            pltpu.VMEM((full_width, width), jnp.bfloat16),
            pltpu.VMEM((n_cand, block_rows, DH), jnp.bfloat16),
            pltpu.VMEM((n_tiles, width, TILE), jnp.bfloat16),
            pltpu.VMEM((n_tiles, width, TILE), jnp.float32),
            pltpu.VMEM((1, 128), jnp.int32),
            pltpu.VMEM((n_cand, 1, 128), jnp.int32),
            pltpu.SMEM((n_cand, 1, 128), jnp.int32),
            pltpu.VMEM((n_cand, score_rows, TILE), jnp.float32),
            pltpu.VMEM((n_head, n_cand, score_rows, TILE), jnp.float32),
            dma((5,)),
            dma((n_head,)),
            dma((n_head,)),
            dma((n_head * n_tiles,)),
            dma((n_head * n_tiles,)),
            dma,
            dma,
            dma,
            dma((n_cand * 4,)),
            dma((n_cand,)),
            dma,
            dma,
        ],
        compiler_params=pltpu.CompilerParams(
            collective_id=0, has_side_effects=True, vmem_limit_bytes=60 * 1024 * 1024
        ),
    )(
        event_feats.reshape(rows, part), item_feats, memory_cache, norm_cache, query_weight, key_weight,
        value_weight, gates_t, input_bias, forget_bias, head_gain, tiles,
    )
    return new_memory, new_norm, scores


def solution(mesh):
    in_specs = (
        P("cand", "head"),
        P("cand", None, "head"),
        P("cand", "head", None, None),
        P("cand", "head", None),
        P(None, "head"),
        P(None, "head"),
        P(None, "head"),
        P(None, None, "head"),
        P("head"),
        P("head"),
        P("head", None),
        P("cand", None, None),
    )
    out_specs = (P("cand", "head", None, None), P("cand", "head", None), P("cand", "head"))
    return jax.shard_map(
        on_device, mesh=mesh, in_specs=in_specs, out_specs=out_specs, check_vma=False
    )
```

```python
import functools
import math

import jax
import jax.numpy as jnp
from jax import lax
from jax.experimental import pallas as pl
from jax.experimental.pallas import tpu as pltpu
from jax.sharding import PartitionSpec as P

DH = 128
TILE = 128
TILES_DEV = 8
TPD = 2
GROUPS = 4
PAD = 32
PIECES = 2
HI = lax.Precision.HIGHEST
MESH = pl.DeviceIdType.MESH


def dot(a, b, precision=None):
    return jnp.dot(a, b, preferred_element_type=jnp.float32, precision=precision)


def kernel(
    n_cand, n_head, users, events, heads, full_width,
    ev_ref, item_ref, mem_ref, nrm_ref, wq_ref, wk_ref, wv_ref, gate_ref, bias_i, bias_f, gain_ref, own_tl,
    nm_ref, nn_ref, sc_ref,
    ev, feats, wq, wk, wv, blocks, queries, weighted, tl_ref, tl_all, tl_s, scores, got,
    in_sem, ev_send, ev_recv, item_send, item_recv, tl_send, tl_recv, tl_sem,
    send_sem, recv_sem, back_send, back_recv,
):
    me = lax.axis_index("cand")
    head = lax.axis_index("head")
    core = me % 2
    col = (me // 2) % 2
    line = me // 4
    n_line = n_cand // 4
    width = heads * DH
    rows = users * events
    n_tiles = feats.shape[1] // TILE
    part = full_width // n_head
    norm_row = users * heads * DH

    def source(z, y, k):
        return z * 4 + y * 2 + k

    loads = [
        pltpu.make_async_copy(ev_ref, ev.at[head], in_sem.at[0]),
        pltpu.make_async_copy(wk_ref, wk, in_sem.at[1]),
        pltpu.make_async_copy(wv_ref, wv, in_sem.at[2]),
        pltpu.make_async_copy(item_ref, feats.at[head], in_sem.at[3]),
        pltpu.make_async_copy(wq_ref, wq, in_sem.at[4]),
    ]
    for load in loads:
        load.start()

    entry = lax.broadcasted_iota(jnp.int32, (1, 128), 1)
    own_row = jnp.zeros((1, 128), jnp.int32)
    for u in range(users):
        for g in range(GROUPS):
            for p in range(TPD):
                own_row = jnp.where(entry == (u * GROUPS + g) * TPD + p, own_tl[u, p, g], own_row)
    tl_ref[...] = own_row

    barrier = pltpu.get_barrier_semaphore()

    def greet(off, carry):
        d = (me * n_head + head + off) % (n_cand * n_head)
        pl.semaphore_signal(
            barrier, inc=1, device_id=(d // n_head, d % n_head), device_id_type=MESH
        )
        return carry

    lax.fori_loop(1, n_cand * n_head, greet, 0)
    pl.semaphore_wait(barrier, n_cand * n_head - 1)

    def ev_copy(off):
        return pltpu.make_async_remote_copy(
            src_ref=ev_ref, dst_ref=ev.at[head], send_sem=ev_send.at[off], recv_sem=ev_recv.at[head],
            device_id=(me, (head + off) % n_head), device_id_type=MESH,
        )

    for off in range(1, n_head):
        ev_copy(off).start()

    def item_copy(off, t):
        at = pl.ds(pl.multiple_of(t * TILE, TILE), TILE)
        return pltpu.make_async_remote_copy(
            src_ref=item_ref.at[at], dst_ref=feats.at[head, at],
            send_sem=item_send.at[off * n_tiles + t], recv_sem=item_recv.at[head * n_tiles + t],
            device_id=(me, (head + off) % n_head), device_id_type=MESH,
        )

    for t in range(n_tiles):
        for off in range(1, n_head):
            item_copy(off, t).start()

    def tl_copy(c):
        return pltpu.make_async_remote_copy(
            src_ref=tl_ref, dst_ref=tl_all.at[me], send_sem=tl_send, recv_sem=tl_recv,
            device_id=(c, head), device_id_type=MESH,
        )

    def send_list(off, carry):
        tl_copy((me + off) % n_cand).start()
        return carry

    lax.fori_loop(1, n_cand, send_list, 0)
    pltpu.make_async_copy(tl_ref, tl_all.at[me], tl_recv).start()

    for off in range(1, n_head):
        src = (head + off) % n_head
        pltpu.make_async_copy(ev.at[src], ev.at[src], ev_recv.at[src]).wait()

    for load in loads[:3]:
        load.wait()
    pre = []
    for bias in (bias_i, bias_f):
        h_id = lax.broadcasted_iota(jnp.int32, (heads, rows), 0)
        column = jnp.zeros((heads, rows), jnp.float32)
        for h in range(heads):
            column = jnp.where(h_id == h, bias[h], column)
        pre.append(column)
    keys = jnp.zeros((rows, width), jnp.float32)
    values = jnp.zeros((rows, width), jnp.float32)
    for hh in range(n_head):
        at = slice(hh * part, (hh + 1) * part)
        x = ev[hh]
        for i in range(2):
            pre[i] += lax.dot_general(
                gate_ref[i, :, at], x, (((1,), (1,)), ((), ())), preferred_element_type=jnp.float32
            )
        keys += dot(x, wk[at, :])
        values += dot(x, wv[at, :])
    keys = keys * (1.0 / math.sqrt(DH))
    values_t = values.T
    forget = pre[1]
    log_forget = jnp.minimum(forget, 0.0) - jnp.log1p(jnp.exp(-jnp.abs(forget)))
    s_id = lax.broadcasted_iota(jnp.int32, (rows, rows), 0)
    t_id = lax.broadcasted_iota(jnp.int32, (rows, rows), 1)
    later = jnp.where((s_id > t_id) & (s_id // events == t_id // events), 1.0, 0.0)
    weight = jax.nn.sigmoid(pre[0]) * jnp.exp(dot(log_forget, later, HI))
    lane_user = lax.broadcasted_iota(jnp.int32, (heads, rows), 1) // events
    norms = []
    for u in range(users):
        mine = lane_user == u
        carry = jnp.exp(jnp.sum(jnp.where(mine, log_forget, 0.0), axis=1, keepdims=True))
        weight_u = jnp.where(mine, weight, 0.0)
        norm_add = dot(weight_u, keys, HI)
        norm_old = nrm_ref[u].astype(jnp.float32)
        for h in range(heads):
            at = slice(h * DH, (h + 1) * DH)
            update = dot(values_t[at, :] * weight_u[h : h + 1, :], keys[:, at], HI)
            new = carry[h : h + 1, :] * mem_ref[u, h].astype(jnp.float32) + update
            r = (u * heads + h) * DH
            blocks[me, r : r + DH, :] = new.astype(jnp.bfloat16)
            norms.append(carry[h : h + 1, :] * norm_old[h : h + 1, :] + norm_add[h : h + 1, at])
    norms.append(jnp.zeros((PAD - users * heads, DH), jnp.float32))
    blocks[me, norm_row : norm_row + PAD, :] = jnp.concatenate(norms, axis=0).astype(jnp.bfloat16)

    piece_rows = blocks.shape[1] // PIECES

    def send(src, q, way, c):
        at = pl.ds(q * piece_rows, piece_rows)
        return pltpu.make_async_remote_copy(
            src_ref=blocks.at[src, at], dst_ref=blocks.at[src, at],
            send_sem=send_sem.at[(src * PIECES + q) * 4 + way], recv_sem=recv_sem.at[src * PIECES + q],
            device_id=(c, head), device_id_type=MESH,
        )

    up = source(jnp.minimum(line + 1, n_line - 1), col, core)
    down = source(jnp.maximum(line - 1, 0), col, core)
    across = source(line, 1 - col, core)
    twin = source(line, col, 1 - core)

    def each_send(z, q, act):
        src = source(z, col, core)
        act(send(src, q, 2, across))

        @pl.when((z <= line) & (line + 1 < n_line))
        def _():
            act(send(src, q, 0, up))

        @pl.when((z >= line) & (line >= 1))
        def _():
            act(send(src, q, 1, down))

        act(send(src, q, 3, twin))

    def start(copy):
        copy.start()

    def arrived(src, q):
        at = pl.ds(q * piece_rows, piece_rows)
        pltpu.make_async_copy(
            blocks.at[src, at], blocks.at[src, at], recv_sem.at[src * PIECES + q]
        ).wait()

    near = jnp.minimum(line, n_line - 1 - line)
    far_sign = jnp.where(line < n_line - 1 - line, 1, -1)

    def order(n):
        paired = line + jnp.where(n % 2 == 1, -1, 1) * ((n + 1) // 2)
        return jnp.where(n <= 2 * near, paired, line + far_sign * (n - near))

    def from_across(n, q):
        src = source(order(n), 1 - col, core)
        arrived(src, q)
        send(src, q, 3, twin).start()

    for q in range(PIECES):
        each_send(line, q, start)

    for u in range(users):
        for h in range(heads):
            r = (u * heads + h) * DH
            nm_ref[u, h] = blocks[me, r : r + DH, :]
    final_norms = blocks[me, norm_row : norm_row + PAD, :].astype(jnp.float32)
    for u in range(users):
        nn_ref[u] = final_norms[u * heads : (u + 1) * heads, :].astype(jnp.bfloat16)

    loads[3].wait()
    loads[4].wait()

    def features(t, carry):
        at = pl.ds(pl.multiple_of(t * TILE, TILE), TILE)
        x = feats[head, at, :].astype(jnp.float32)
        for h in range(heads):
            c = slice(h * DH, (h + 1) * DH)
            weighted[t, c, :] = (x[:, c] * (gain_ref[h : h + 1, :] * (1.0 / math.sqrt(full_width)))).T
        return carry

    lax.fori_loop(0, n_tiles, features, 0)

    def project(t, carry):
        at = pl.ds(pl.multiple_of(t * TILE, TILE), TILE)
        for off in range(1, n_head):
            src = (head + off) % n_head
            pltpu.make_async_copy(
                feats.at[src, at], feats.at[src, at], item_recv.at[src * n_tiles + t]
            ).wait()
        acc = jnp.zeros((TILE, width), jnp.float32)
        for hh in range(n_head):
            acc += dot(feats[hh, at, :], wq[hh * part : (hh + 1) * part, :])
        acc = acc * (1.0 / math.sqrt(DH))
        for h in range(heads):
            c = slice(h * DH, (h + 1) * DH)
            queries[t, c, :] = acc[:, c].T.astype(jnp.bfloat16)
        return carry

    lax.fori_loop(0, n_tiles // n_line, project, 0)
    for s in range(1, n_line):

        for q in range(PIECES):

            @pl.when(line - s >= 0)
            def _():
                arrived(source(line - s, col, core), q)
                each_send(line - s, q, start)

            @pl.when(line + s < n_line)
            def _():
                arrived(source(line + s, col, core), q)
                each_send(line + s, q, start)

            from_across(jnp.int32(s - 1), q)
        lax.fori_loop(s * n_tiles // n_line, (s + 1) * n_tiles // n_line, project, 0)

    pltpu.make_async_copy(tl_all, tl_all, tl_recv).wait()
    to_smem = pltpu.make_async_copy(tl_all, tl_s, tl_sem)
    to_smem.start()
    to_smem.wait()

    def back_copy(src, h):
        return pltpu.make_async_remote_copy(
            src_ref=scores.at[src], dst_ref=got.at[head, me], send_sem=back_send, recv_sem=back_recv,
            device_id=(src, h), device_id_type=MESH,
        )

    def score(j, carry):
        @pl.when(j == 2 * n_line)
        def _():
            for q in range(PIECES):
                from_across(jnp.int32(n_line - 1), q)

        z = order(j % n_line)
        y = jnp.where(j < 2 * n_line, col, 1 - col)
        other = (j // n_line) % 2
        k = jnp.where(other == 0, core, 1 - core)
        src = source(z, y, k)

        @pl.when(other == 1)
        def _():
            for q in range(PIECES):
                arrived(src, q)

        norm_block = blocks[src, norm_row : norm_row + PAD // 2, :]
        for u in range(users):
            picks = [jnp.int32(0), jnp.int32(0)]
            for g in range(GROUPS):
                first = tl_s[src, 0, (u * GROUPS + g) * TPD]
                hit = first // TILES_DEV == me
                for p in range(TPD):
                    tile = tl_s[src, 0, (u * GROUPS + g) * TPD + p]
                    picks[p] = jnp.where(hit, tile % TILES_DEV, picks[p])
            totals = [jnp.zeros((1, TILE), jnp.float32) for _ in range(TPD)]
            for h in range(heads):
                r = (u * heads + h) * DH
                left = jnp.concatenate([blocks[src, r : r + DH, :], norm_block], axis=0)
                c = slice(h * DH, (h + 1) * DH)
                for p in range(TPD):
                    product = dot(left, queries[picks[p], c, :])
                    numer = product[:DH]
                    i = DH + u * heads + h
                    denom = product[i : i + 1]
                    square = jnp.sum(numer * numer, axis=0, keepdims=True)
                    value = jnp.sum(numer * weighted[picks[p], c, :], axis=0, keepdims=True)
                    totals[p] += value * lax.rsqrt(square * (1.0 / DH) + 1e-05) / jnp.maximum(
                        jnp.abs(denom), 1.0
                    )
            for p in range(TPD):
                scores[src, u * TPD + p : u * TPD + p + 1, :] = totals[p]
        for h in range(n_head):
            here = (src == me) & (head == h)

            @pl.when(here)
            def _():
                pltpu.make_async_copy(scores.at[src], got.at[head, me], back_recv).start()

            @pl.when(jnp.logical_not(here))
            def _():
                back_copy(src, h).start()

        return carry

    lax.fori_loop(0, n_cand, score, 0)

    pltpu.make_async_copy(got, got, back_recv).wait()
    n_cols = GROUPS * TPD // n_head
    for u in range(users):
        for q in range(n_cols):
            m = head * n_cols + q
            first = own_tl[u, 0, m // TPD]
            block = first // TILES_DEV
            total = jnp.zeros((TPD, TILE), jnp.float32)
            for hh in range(n_head):
                total += got[hh, block][u * TPD : (u + 1) * TPD]
            row = jnp.where(m % TPD == 0, total[0:1], total[1:2])
            sc_ref[u : u + 1, q * TILE : (q + 1) * TILE] = row

    for off in range(1, n_head):
        ev_copy(off).wait_send()

    def item_left(t, carry):
        for off in range(1, n_head):
            item_copy(off, t).wait_send()
        return carry

    lax.fori_loop(0, n_tiles, item_left, 0)
    rest = pl.ds(0, n_cand - 1)
    pltpu.make_async_copy(tl_all.at[rest], tl_all.at[rest], tl_send).wait()

    def left(copy):
        copy.wait_send()

    def blocks_left(z, carry):
        for q in range(PIECES):
            each_send(z, q, left)
            send(source(z, 1 - col, core), q, 3, twin).wait_send()
        return carry

    lax.fori_loop(0, n_line, blocks_left, 0)
    for h in range(n_head):
        here = head == h

        @pl.when(here)
        def _():
            pltpu.make_async_copy(scores.at[rest], scores.at[rest], back_send).wait()

        @pl.when(jnp.logical_not(here))
        def _():
            pltpu.make_async_copy(scores, scores, back_send).wait()


def on_device(
    item_feats, event_feats, memory_cache, norm_cache, query_weight, key_weight, value_weight,
    gate_weight, input_bias, forget_bias, head_gain, tile_list,
):
    n_cand = lax.axis_size("cand")
    n_head = lax.axis_size("head")
    users, events, part = event_feats.shape
    heads = memory_cache.shape[1]
    full_width, width = query_weight.shape
    pool = item_feats.shape[0]
    n_tiles = pool // TILE
    rows = users * events
    gates_t = jnp.transpose(gate_weight, (0, 2, 1))
    tiles = jnp.transpose(tile_list, (0, 2, 1))
    block_rows = users * heads * DH + PAD
    score_rows = max(8, users * TPD)
    vmem = pl.BlockSpec(memory_space=pltpu.VMEM)
    smem = pl.BlockSpec(memory_space=pltpu.SMEM)
    any_space = pl.BlockSpec(memory_space=pltpu.HBM)
    dma = pltpu.SemaphoreType.DMA
    new_memory, new_norm, scores = pl.pallas_call(
        functools.partial(kernel, n_cand, n_head, users, events, heads, full_width),
        out_shape=(
            jax.ShapeDtypeStruct(memory_cache.shape, jnp.bfloat16),
            jax.ShapeDtypeStruct(norm_cache.shape, jnp.bfloat16),
            jax.ShapeDtypeStruct((users, GROUPS * TPD * TILE // n_head), jnp.float32),
        ),
        in_specs=[any_space, any_space, vmem, vmem, any_space, any_space, any_space, vmem, smem, smem, vmem, smem],
        out_specs=(vmem, vmem, vmem),
        scratch_shapes=[
            pltpu.VMEM((n_head, rows, part), jnp.bfloat16),
            pltpu.VMEM((n_head, pool, part), jnp.bfloat16),
            pltpu.VMEM((full_width, width), jnp.bfloat16),
            pltpu.VMEM((full_width, width), jnp.bfloat16),
            pltpu.VMEM((full_width, width), jnp.bfloat16),
            pltpu.VMEM((n_cand, block_rows, DH), jnp.bfloat16),
            pltpu.VMEM((n_tiles, width, TILE), jnp.bfloat16),
            pltpu.VMEM((n_tiles, width, TILE), jnp.float32),
            pltpu.VMEM((1, 128), jnp.int32),
            pltpu.VMEM((n_cand, 1, 128), jnp.int32),
            pltpu.SMEM((n_cand, 1, 128), jnp.int32),
            pltpu.VMEM((n_cand, score_rows, TILE), jnp.float32),
            pltpu.VMEM((n_head, n_cand, score_rows, TILE), jnp.float32),
            dma((5,)),
            dma((n_head,)),
            dma((n_head,)),
            dma((n_head * n_tiles,)),
            dma((n_head * n_tiles,)),
            dma,
            dma,
            dma,
            dma((n_cand * PIECES * 4,)),
            dma((n_cand * PIECES,)),
            dma,
            dma,
        ],
        compiler_params=pltpu.CompilerParams(
            collective_id=0, has_side_effects=True, vmem_limit_bytes=60 * 1024 * 1024
        ),
    )(
        event_feats.reshape(rows, part), item_feats, memory_cache, norm_cache, query_weight, key_weight,
        value_weight, gates_t, input_bias, forget_bias, head_gain, tiles,
    )
    return new_memory, new_norm, scores


def solution(mesh):
    in_specs = (
        P("cand", "head"),
        P("cand", None, "head"),
        P("cand", "head", None, None),
        P("cand", "head", None),
        P(None, "head"),
        P(None, "head"),
        P(None, "head"),
        P(None, None, "head"),
        P("head"),
        P("head"),
        P("head", None),
        P("cand", None, None),
    )
    out_specs = (P("cand", "head", None, None), P("cand", "head", None), P("cand", "head"))
    return jax.shard_map(
        on_device, mesh=mesh, in_specs=in_specs, out_specs=out_specs, check_vma=False
    )
```

```python
import functools
import math

import jax
import jax.numpy as jnp
from jax import lax
from jax.experimental import pallas as pl
from jax.experimental.pallas import tpu as pltpu
from jax.sharding import PartitionSpec as P

DH = 128
TILE = 128
TILES_DEV = 8
TPD = 2
GROUPS = 4
PAD = 32
PIECES = 2
HI = lax.Precision.HIGHEST
MESH = pl.DeviceIdType.MESH


def dot(a, b, precision=None):
    return jnp.dot(a, b, preferred_element_type=jnp.float32, precision=precision)


def kernel(
    n_cand, n_head, users, events, heads, full_width,
    ev_ref, item_ref, mem_ref, nrm_ref, wq_ref, wk_ref, wv_ref, gate_ref, bias_i, bias_f, gain_ref, own_tl,
    nm_ref, nn_ref, sc_ref,
    ev, feats, wq, wk, wv, blocks, queries, weighted, tl_ref, tl_all, tl_s, scores, got,
    in_sem, ev_send, ev_recv, item_send, item_recv, tl_send, tl_recv, tl_sem,
    send_sem, recv_sem, back_send, back_recv,
):
    me = lax.axis_index("cand")
    head = lax.axis_index("head")
    core = me % 2
    col = (me // 2) % 2
    line = me // 4
    n_line = n_cand // 4
    width = heads * DH
    rows = users * events
    n_tiles = feats.shape[1] // TILE
    part = full_width // n_head
    norm_row = users * heads * DH

    def source(z, y, k):
        return z * 4 + y * 2 + k

    loads = [
        pltpu.make_async_copy(ev_ref, ev.at[head], in_sem.at[0]),
        pltpu.make_async_copy(wk_ref, wk, in_sem.at[1]),
        pltpu.make_async_copy(wv_ref, wv, in_sem.at[2]),
        pltpu.make_async_copy(item_ref, feats.at[head], in_sem.at[3]),
        pltpu.make_async_copy(wq_ref, wq, in_sem.at[4]),
    ]
    for load in loads:
        load.start()

    entry = lax.broadcasted_iota(jnp.int32, (1, 128), 1)
    own_row = jnp.zeros((1, 128), jnp.int32)
    for u in range(users):
        for g in range(GROUPS):
            for p in range(TPD):
                own_row = jnp.where(entry == (u * GROUPS + g) * TPD + p, own_tl[u, p, g], own_row)
    tl_ref[...] = own_row

    barrier = pltpu.get_barrier_semaphore()

    def greet(off, carry):
        d = (me * n_head + head + off) % (n_cand * n_head)
        pl.semaphore_signal(
            barrier, inc=1, device_id=(d // n_head, d % n_head), device_id_type=MESH
        )
        return carry

    lax.fori_loop(1, n_cand * n_head, greet, 0)

    for load in loads[:3]:
        load.wait()
    pre = []
    for bias in (bias_i, bias_f):
        h_id = lax.broadcasted_iota(jnp.int32, (heads, rows), 0)
        column = jnp.zeros((heads, rows), jnp.float32)
        for h in range(heads):
            column = jnp.where(h_id == h, bias[h], column)
        pre.append(column)
    sums = [pre, jnp.zeros((rows, width), jnp.float32), jnp.zeros((rows, width), jnp.float32)]

    def add_half(src):
        at = pl.ds(pl.multiple_of(src * part, 128), part)
        x = ev[src]
        for i in range(2):
            sums[0][i] += lax.dot_general(
                gate_ref[i, :, at], x, (((1,), (1,)), ((), ())), preferred_element_type=jnp.float32
            )
        sums[1] += dot(x, wk[at, :])
        sums[2] += dot(x, wv[at, :])

    add_half(head)
    pl.semaphore_wait(barrier, n_cand * n_head - 1)

    def ev_copy(off):
        return pltpu.make_async_remote_copy(
            src_ref=ev_ref, dst_ref=ev.at[head], send_sem=ev_send.at[off], recv_sem=ev_recv.at[head],
            device_id=(me, (head + off) % n_head), device_id_type=MESH,
        )

    for off in range(1, n_head):
        ev_copy(off).start()

    def item_copy(off, t):
        at = pl.ds(pl.multiple_of(t * TILE, TILE), TILE)
        return pltpu.make_async_remote_copy(
            src_ref=item_ref.at[at], dst_ref=feats.at[head, at],
            send_sem=item_send.at[off * n_tiles + t], recv_sem=item_recv.at[head * n_tiles + t],
            device_id=(me, (head + off) % n_head), device_id_type=MESH,
        )

    for t in range(n_tiles):
        for off in range(1, n_head):
            item_copy(off, t).start()

    def tl_copy(c):
        return pltpu.make_async_remote_copy(
            src_ref=tl_ref, dst_ref=tl_all.at[me], send_sem=tl_send, recv_sem=tl_recv,
            device_id=(c, head), device_id_type=MESH,
        )

    def send_list(off, carry):
        tl_copy((me + off) % n_cand).start()
        return carry

    lax.fori_loop(1, n_cand, send_list, 0)
    pltpu.make_async_copy(tl_ref, tl_all.at[me], tl_recv).start()

    for off in range(1, n_head):
        src = (head + off) % n_head
        pltpu.make_async_copy(ev.at[src], ev.at[src], ev_recv.at[src]).wait()

    for off in range(1, n_head):
        add_half((head + off) % n_head)
    pre, keys, values = sums
    keys = keys * (1.0 / math.sqrt(DH))
    values_t = values.T
    forget = pre[1]
    log_forget = jnp.minimum(forget, 0.0) - jnp.log1p(jnp.exp(-jnp.abs(forget)))
    s_id = lax.broadcasted_iota(jnp.int32, (rows, rows), 0)
    t_id = lax.broadcasted_iota(jnp.int32, (rows, rows), 1)
    later = jnp.where((s_id > t_id) & (s_id // events == t_id // events), 1.0, 0.0)
    weight = jax.nn.sigmoid(pre[0]) * jnp.exp(dot(log_forget, later, HI))
    lane_user = lax.broadcasted_iota(jnp.int32, (heads, rows), 1) // events
    norms = []
    for u in range(users):
        mine = lane_user == u
        carry = jnp.exp(jnp.sum(jnp.where(mine, log_forget, 0.0), axis=1, keepdims=True))
        weight_u = jnp.where(mine, weight, 0.0)
        norm_add = dot(weight_u, keys, HI)
        norm_old = nrm_ref[u].astype(jnp.float32)
        for h in range(heads):
            at = slice(h * DH, (h + 1) * DH)
            update = dot(values_t[at, :] * weight_u[h : h + 1, :], keys[:, at], HI)
            new = carry[h : h + 1, :] * mem_ref[u, h].astype(jnp.float32) + update
            r = (u * heads + h) * DH
            blocks[me, r : r + DH, :] = new.astype(jnp.bfloat16)
            norms.append(carry[h : h + 1, :] * norm_old[h : h + 1, :] + norm_add[h : h + 1, at])
    norms.append(jnp.zeros((PAD - users * heads, DH), jnp.float32))
    blocks[me, norm_row : norm_row + PAD, :] = jnp.concatenate(norms, axis=0).astype(jnp.bfloat16)

    piece_rows = blocks.shape[1] // PIECES

    def send(src, q, way, c):
        at = pl.ds(q * piece_rows, piece_rows)
        return pltpu.make_async_remote_copy(
            src_ref=blocks.at[src, at], dst_ref=blocks.at[src, at],
            send_sem=send_sem.at[(src * PIECES + q) * 4 + way], recv_sem=recv_sem.at[src * PIECES + q],
            device_id=(c, head), device_id_type=MESH,
        )

    up = source(jnp.minimum(line + 1, n_line - 1), col, core)
    down = source(jnp.maximum(line - 1, 0), col, core)
    across = source(line, 1 - col, core)
    twin = source(line, col, 1 - core)

    def each_send(z, q, act):
        src = source(z, col, core)
        act(send(src, q, 2, across))

        @pl.when((z <= line) & (line + 1 < n_line))
        def _():
            act(send(src, q, 0, up))

        @pl.when((z >= line) & (line >= 1))
        def _():
            act(send(src, q, 1, down))

        act(send(src, q, 3, twin))

    def start(copy):
        copy.start()

    def arrived(src, q):
        at = pl.ds(q * piece_rows, piece_rows)
        pltpu.make_async_copy(
            blocks.at[src, at], blocks.at[src, at], recv_sem.at[src * PIECES + q]
        ).wait()

    near = jnp.minimum(line, n_line - 1 - line)
    far_sign = jnp.where(line < n_line - 1 - line, 1, -1)

    def order(n):
        paired = line + jnp.where(n % 2 == 1, -1, 1) * ((n + 1) // 2)
        return jnp.where(n <= 2 * near, paired, line + far_sign * (n - near))

    def from_across(n, q):
        src = source(order(n), 1 - col, core)
        arrived(src, q)
        send(src, q, 3, twin).start()

    for q in range(PIECES):
        each_send(line, q, start)

    for u in range(users):
        for h in range(heads):
            r = (u * heads + h) * DH
            nm_ref[u, h] = blocks[me, r : r + DH, :]
    final_norms = blocks[me, norm_row : norm_row + PAD, :].astype(jnp.float32)
    for u in range(users):
        nn_ref[u] = final_norms[u * heads : (u + 1) * heads, :].astype(jnp.bfloat16)

    loads[3].wait()
    loads[4].wait()

    def features(t, carry):
        at = pl.ds(pl.multiple_of(t * TILE, TILE), TILE)
        x = feats[head, at, :].astype(jnp.float32)
        for h in range(heads):
            c = slice(h * DH, (h + 1) * DH)
            weighted[t, c, :] = (x[:, c] * (gain_ref[h : h + 1, :] * (1.0 / math.sqrt(full_width)))).T
        return carry

    lax.fori_loop(0, n_tiles, features, 0)

    def project(t, carry):
        at = pl.ds(pl.multiple_of(t * TILE, TILE), TILE)
        for off in range(1, n_head):
            src = (head + off) % n_head
            pltpu.make_async_copy(
                feats.at[src, at], feats.at[src, at], item_recv.at[src * n_tiles + t]
            ).wait()
        acc = jnp.zeros((TILE, width), jnp.float32)
        for hh in range(n_head):
            acc += dot(feats[hh, at, :], wq[hh * part : (hh + 1) * part, :])
        acc = acc * (1.0 / math.sqrt(DH))
        for h in range(heads):
            c = slice(h * DH, (h + 1) * DH)
            queries[t, c, :] = acc[:, c].T.astype(jnp.bfloat16)
        return carry

    lax.fori_loop(0, n_tiles // n_line, project, 0)
    for s in range(1, n_line):

        for q in range(PIECES):

            @pl.when(line - s >= 0)
            def _():
                arrived(source(line - s, col, core), q)
                each_send(line - s, q, start)

            @pl.when(line + s < n_line)
            def _():
                arrived(source(line + s, col, core), q)
                each_send(line + s, q, start)

            from_across(jnp.int32(s - 1), q)
        lax.fori_loop(s * n_tiles // n_line, (s + 1) * n_tiles // n_line, project, 0)

    pltpu.make_async_copy(tl_all, tl_all, tl_recv).wait()
    to_smem = pltpu.make_async_copy(tl_all, tl_s, tl_sem)
    to_smem.start()
    to_smem.wait()

    def back_copy(src, h):
        return pltpu.make_async_remote_copy(
            src_ref=scores.at[src], dst_ref=got.at[head, me], send_sem=back_send, recv_sem=back_recv,
            device_id=(src, h), device_id_type=MESH,
        )

    def score(j, carry):
        @pl.when(j == 2 * n_line)
        def _():
            for q in range(PIECES):
                from_across(jnp.int32(n_line - 1), q)

        z = order(j % n_line)
        y = jnp.where(j < 2 * n_line, col, 1 - col)
        other = (j // n_line) % 2
        k = jnp.where(other == 0, core, 1 - core)
        src = source(z, y, k)

        @pl.when(other == 1)
        def _():
            for q in range(PIECES):
                arrived(src, q)

        norm_block = blocks[src, norm_row : norm_row + PAD // 2, :]
        for u in range(users):
            picks = [jnp.int32(0), jnp.int32(0)]
            for g in range(GROUPS):
                first = tl_s[src, 0, (u * GROUPS + g) * TPD]
                hit = first // TILES_DEV == me
                for p in range(TPD):
                    tile = tl_s[src, 0, (u * GROUPS + g) * TPD + p]
                    picks[p] = jnp.where(hit, tile % TILES_DEV, picks[p])
            totals = [jnp.zeros((1, TILE), jnp.float32) for _ in range(TPD)]
            for h in range(heads):
                r = (u * heads + h) * DH
                left = jnp.concatenate([blocks[src, r : r + DH, :], norm_block], axis=0)
                c = slice(h * DH, (h + 1) * DH)
                for p in range(TPD):
                    product = dot(left, queries[picks[p], c, :])
                    numer = product[:DH]
                    i = DH + u * heads + h
                    denom = product[i : i + 1]
                    square = jnp.sum(numer * numer, axis=0, keepdims=True)
                    value = jnp.sum(numer * weighted[picks[p], c, :], axis=0, keepdims=True)
                    totals[p] += value * lax.rsqrt(square * (1.0 / DH) + 1e-05) / jnp.maximum(
                        jnp.abs(denom), 1.0
                    )
            for p in range(TPD):
                scores[src, u * TPD + p : u * TPD + p + 1, :] = totals[p]
        for h in range(n_head):
            here = (src == me) & (head == h)

            @pl.when(here)
            def _():
                pltpu.make_async_copy(scores.at[src], got.at[head, me], back_recv).start()

            @pl.when(jnp.logical_not(here))
            def _():
                back_copy(src, h).start()

        return carry

    lax.fori_loop(0, n_cand, score, 0)

    pltpu.make_async_copy(got, got, back_recv).wait()
    n_cols = GROUPS * TPD // n_head
    for u in range(users):
        for q in range(n_cols):
            m = head * n_cols + q
            first = own_tl[u, 0, m // TPD]
            block = first // TILES_DEV
            total = jnp.zeros((TPD, TILE), jnp.float32)
            for hh in range(n_head):
                total += got[hh, block][u * TPD : (u + 1) * TPD]
            row = jnp.where(m % TPD == 0, total[0:1], total[1:2])
            sc_ref[u : u + 1, q * TILE : (q + 1) * TILE] = row

    for off in range(1, n_head):
        ev_copy(off).wait_send()

    def item_left(t, carry):
        for off in range(1, n_head):
            item_copy(off, t).wait_send()
        return carry

    lax.fori_loop(0, n_tiles, item_left, 0)
    rest = pl.ds(0, n_cand - 1)
    pltpu.make_async_copy(tl_all.at[rest], tl_all.at[rest], tl_send).wait()

    def left(copy):
        copy.wait_send()

    def blocks_left(z, carry):
        for q in range(PIECES):
            each_send(z, q, left)
            send(source(z, 1 - col, core), q, 3, twin).wait_send()
        return carry

    lax.fori_loop(0, n_line, blocks_left, 0)
    for h in range(n_head):
        here = head == h

        @pl.when(here)
        def _():
            pltpu.make_async_copy(scores.at[rest], scores.at[rest], back_send).wait()

        @pl.when(jnp.logical_not(here))
        def _():
            pltpu.make_async_copy(scores, scores, back_send).wait()


def on_device(
    item_feats, event_feats, memory_cache, norm_cache, query_weight, key_weight, value_weight,
    gate_weight, input_bias, forget_bias, head_gain, tile_list,
):
    n_cand = lax.axis_size("cand")
    n_head = lax.axis_size("head")
    users, events, part = event_feats.shape
    heads = memory_cache.shape[1]
    full_width, width = query_weight.shape
    pool = item_feats.shape[0]
    n_tiles = pool // TILE
    rows = users * events
    gates_t = jnp.transpose(gate_weight, (0, 2, 1))
    tiles = jnp.transpose(tile_list, (0, 2, 1))
    block_rows = users * heads * DH + PAD
    score_rows = max(8, users * TPD)
    vmem = pl.BlockSpec(memory_space=pltpu.VMEM)
    smem = pl.BlockSpec(memory_space=pltpu.SMEM)
    any_space = pl.BlockSpec(memory_space=pltpu.HBM)
    dma = pltpu.SemaphoreType.DMA
    new_memory, new_norm, scores = pl.pallas_call(
        functools.partial(kernel, n_cand, n_head, users, events, heads, full_width),
        out_shape=(
            jax.ShapeDtypeStruct(memory_cache.shape, jnp.bfloat16),
            jax.ShapeDtypeStruct(norm_cache.shape, jnp.bfloat16),
            jax.ShapeDtypeStruct((users, GROUPS * TPD * TILE // n_head), jnp.float32),
        ),
        in_specs=[any_space, any_space, vmem, vmem, any_space, any_space, any_space, vmem, smem, smem, vmem, smem],
        out_specs=(vmem, vmem, vmem),
        scratch_shapes=[
            pltpu.VMEM((n_head, rows, part), jnp.bfloat16),
            pltpu.VMEM((n_head, pool, part), jnp.bfloat16),
            pltpu.VMEM((full_width, width), jnp.bfloat16),
            pltpu.VMEM((full_width, width), jnp.bfloat16),
            pltpu.VMEM((full_width, width), jnp.bfloat16),
            pltpu.VMEM((n_cand, block_rows, DH), jnp.bfloat16),
            pltpu.VMEM((n_tiles, width, TILE), jnp.bfloat16),
            pltpu.VMEM((n_tiles, width, TILE), jnp.float32),
            pltpu.VMEM((1, 128), jnp.int32),
            pltpu.VMEM((n_cand, 1, 128), jnp.int32),
            pltpu.SMEM((n_cand, 1, 128), jnp.int32),
            pltpu.VMEM((n_cand, score_rows, TILE), jnp.float32),
            pltpu.VMEM((n_head, n_cand, score_rows, TILE), jnp.float32),
            dma((5,)),
            dma((n_head,)),
            dma((n_head,)),
            dma((n_head * n_tiles,)),
            dma((n_head * n_tiles,)),
            dma,
            dma,
            dma,
            dma((n_cand * PIECES * 4,)),
            dma((n_cand * PIECES,)),
            dma,
            dma,
        ],
        compiler_params=pltpu.CompilerParams(
            collective_id=0, has_side_effects=True, vmem_limit_bytes=60 * 1024 * 1024
        ),
    )(
        event_feats.reshape(rows, part), item_feats, memory_cache, norm_cache, query_weight, key_weight,
        value_weight, gates_t, input_bias, forget_bias, head_gain, tiles,
    )
    return new_memory, new_norm, scores


def solution(mesh):
    in_specs = (
        P("cand", "head"),
        P("cand", None, "head"),
        P("cand", "head", None, None),
        P("cand", "head", None),
        P(None, "head"),
        P(None, "head"),
        P(None, "head"),
        P(None, None, "head"),
        P("head"),
        P("head"),
        P("head", None),
        P("cand", None, None),
    )
    out_specs = (P("cand", "head", None, None), P("cand", "head", None), P("cand", "head"))
    return jax.shard_map(
        on_device, mesh=mesh, in_specs=in_specs, out_specs=out_specs, check_vma=False
    )
```
